32 devices in a mesh: out: 4 (over x, core), in: 8 (over z, y).
Axes of the slice: x: 2, y: 2, z: 4, core: 2. Of those that a mesh axis runs over, the one named last changes fastest.
Arguments:
- cotangent: bfloat16 [2048, 16384], P('in', 'out'), may hold values from -25.588427 to 25.588427
- activations: bfloat16 [2048, 16384], P('out', 'in'), may hold values from -1158 to 1158
- basis_out: bfloat16 [16384, 1024], P('out'), may hold values from -1 to 1, as said below
- basis_in: bfloat16 [16384, 1024], P('in'), may hold values from -1 to 1, as said below
Outputs:
- projected: float32 [16384, 16384], P('out', 'in')
The draws below stay inside these ranges and needn't reach their ends.
Inputs may be any that keep to these rules, and one draw needn't show every extreme that they name: The columns of basis_out are orthonormal before rounding to bfloat16. The columns of basis_in are orthonormal before rounding to bfloat16.
All inputs are finite; a program needn't handle non-finite values.
Results may differ from the reference program's by a relative error of at most 0.018.
Values may be sent and summed in bfloat16 or wider, within the bound.
No kernel may reach another device: no remote copies, remote signals or barrier semaphores. Data moves between devices by JAX's collectives and lax.ppermute only.
A program may use at most 128 MiB of HBM per device.

```python
import math
import jax
import jax.numpy as jnp
from jax import lax

OUT = 16384
IN = 16384
RANK = 1024
TOKENS = 2048


def basis_matrix(key, row_total, stream):
    sub_key = jax.random.fold_in(key, stream)
    sample = jax.random.normal(sub_key, (row_total, RANK), jnp.float32)
    orthonormal, triangle = jnp.linalg.qr(sample)
    return orthonormal


def noise_field(key, stream, extent):
    sub_key = jax.random.fold_in(key, stream)
    return jax.random.truncated_normal(sub_key, -6.0, 6.0, extent, jnp.float32)


def draw_cotangent(key, part):
    strength = 5.0
    basis_rows = basis_matrix(key, OUT, 11)
    inside = jnp.dot(noise_field(key, 22, (TOKENS, RANK)), basis_rows.T, precision=lax.Precision.HIGHEST)
    result = (noise_field(key, 21, (TOKENS, OUT)) + strength * inside) / math.sqrt(TOKENS)
    return result.astype(jnp.bfloat16)


def draw_activations(key, part):
    strength = 5.0
    basis_rows = basis_matrix(key, IN, 12)
    inside = jnp.dot(noise_field(key, 32, (TOKENS, RANK)), basis_rows.T, precision=lax.Precision.HIGHEST)
    result = noise_field(key, 31, (TOKENS, IN)) + strength * inside
    return result.astype(jnp.bfloat16)


def draw_basis_out(key, part):
    return basis_matrix(key, OUT, 11).astype(jnp.bfloat16)


def draw_basis_in(key, part):
    return basis_matrix(key, IN, 12).astype(jnp.bfloat16)


def setup_inputs(seed: int = 0) -> dict:
    splits = jax.random.split(jax.random.key(seed), 5)
    cotangent = draw_cotangent(jax.random.fold_in(splits[4], 71), 0)
    activations = draw_activations(jax.random.fold_in(splits[4], 71), 0)
    basis_out = draw_basis_out(jax.random.fold_in(splits[4], 71), 0)
    basis_in = draw_basis_in(jax.random.fold_in(splits[4], 71), 0)
    return dict(cotangent=cotangent, activations=activations, basis_out=basis_out, basis_in=basis_in)


def reference(cotangent, activations, basis_out, basis_in):
    gradient = lax.dot_general(cotangent.astype(jnp.float32), activations.astype(jnp.float32), (((0,), (0,)), ((), ())), preferred_element_type=jnp.float32)
    gradient_low = gradient.astype(jnp.bfloat16)
    compressed = jnp.dot(gradient_low.astype(jnp.float32), basis_in.astype(jnp.float32), preferred_element_type=jnp.float32)
    core_matrix = lax.dot_general(basis_out.astype(jnp.float32), compressed.astype(jnp.bfloat16).astype(jnp.float32), (((0,), (0,)), ((), ())), preferred_element_type=jnp.float32)
    expansion = jnp.dot(basis_out.astype(jnp.float32), core_matrix.astype(jnp.bfloat16).astype(jnp.float32), preferred_element_type=jnp.float32).astype(jnp.bfloat16)
    removal = lax.dot_general(expansion.astype(jnp.float32), basis_in.astype(jnp.float32), (((1,), (1,)), ((), ())), preferred_element_type=jnp.float32)
    return gradient - removal
```

```python
import functools

import jax
import jax.numpy as jnp
from jax import lax
from jax.experimental import pallas as pl
from jax.experimental.pallas import tpu as pltpu
from jax.sharding import PartitionSpec as P

FIRST = (((0,), (0,)), ((), ()))
LAST = (((1,), (1,)), ((), ()))
F32, BF16 = jnp.float32, jnp.bfloat16
LANES = 128
PARTS = (1, 1, 2, 2, 1, 1)
FIRST_EVENTS = ("r0", "r1", "q0", "p0", "r0", "q1", "p1", "r1", "q2", "p2", "r0", "c0", "r1", "c1", "r0", "r2", "c2", "r1", "r3", "c3", "f")
LATER_EVENTS = (
    "m0", "r2", "r3", "m1", "r2", "r3", "r2", "r4", "r3", "r4", "r5", "m2", "r4", "r5", "r4", "m3", "r5", "r5", "m4", "m5",
)


def grid_of(mesh):
    count = mesh.shape["in"]
    places = [d.coords for d in mesh.devices[0]]
    wide = sum(p[2] == places[0][2] for p in places)
    return count // wide, wide


def ring_order(tall, wide):
    if wide < 2 or tall % 2:
        return list(range(tall * wide))
    order = []
    for row in range(tall):
        columns = range(1, wide) if row % 2 == 0 else range(wide - 1, 0, -1)
        order += [row * wide + column for column in columns]
    return order + [row * wide for row in reversed(range(tall))]


def after(x, *others):
    return lax.optimization_barrier((x, *others))[0]


def column_specs(x, block, entries, rows, row_of):
    return [x] * len(entries), [
        pl.BlockSpec((rows, block), functools.partial(lambda e, i, t: (row_of(i), t[e]), e)) for e in entries
    ]


def call(kernel, table, operands, specs, shape, dtype, block, index, steps, flops, total=None):
    aliases = {}
    if total is not None:
        operands, specs = [*operands, total], [*specs, pl.BlockSpec(memory_space=pl.ANY)]
        aliases = {len(operands): 0}
    moved = sum(o.size * o.dtype.itemsize for o in operands[:2])
    return pl.pallas_call(
        kernel,
        out_shape=jax.ShapeDtypeStruct(shape, dtype),
        grid_spec=pltpu.PrefetchScalarGridSpec(
            num_scalar_prefetch=1, grid=(steps,), in_specs=specs, out_specs=pl.BlockSpec(block, index)
        ),
        input_output_aliases=aliases,
        compiler_params=pltpu.CompilerParams(vmem_limit_bytes=40 * 2**20),
        cost_estimate=pl.CostEstimate(flops=flops, bytes_accessed=moved, transcendentals=0),
    )(table, *operands)


def body(tall, wide, cotangent, activations, basis_out, basis_in):
    order = ring_order(tall, wide)
    ring, outs = tall * wide, lax.axis_size("out")
    tokens, height = cotangent.shape
    width, rank = basis_in.shape
    all_tokens = tokens * ring
    mine, here = lax.axis_index("out"), lax.axis_index("in")
    row, column = here // wide, here % wide

    place = jnp.asarray([order.index(i) for i in range(ring)], jnp.int32)[here]
    hops = jnp.asarray([0] + [d for s in range(1, ring // 2) for d in (-s, s)] + [ring // 2], jnp.int32)
    hop = jnp.asarray(order, jnp.int32)[(place + hops + ring) % ring]
    steps = [(a, b) for b in range(wide) for a in range(tall)]
    rows_back = (row - jnp.asarray([a for a, _ in steps], jnp.int32) + tall) % tall
    columns_back = (column - jnp.asarray([b for _, b in steps], jnp.int32) + wide) % wide
    held = rows_back * wide + columns_back
    per = ring // outs
    held_slot = ((held // per) ^ mine) * per + held % per
    in_block = columns_back * tall + rows_back
    out_block = jnp.arange(outs, dtype=jnp.int32) ^ mine
    in_share, out_share = rank // ring, rank // outs

    def turn_rows(x, k):
        return lax.ppermute(x, "in", [(a * wide + b, (a + k) % tall * wide + b) for a in range(tall) for b in range(wide)])

    def turn_columns(x, k):
        return lax.ppermute(x, "in", [(a * wide + b, a * wide + (b + k) % wide) for a in range(tall) for b in range(wide)])

    def swap(x, k):
        return lax.ppermute(x, "out", [(i, i ^ k) for i in range(outs)])

    forward = [(order[k], order[(k + 1) % ring]) for k in range(ring)]
    backward = [(b, a) for a, b in forward]

    def part_of(x, block, size):
        return lax.dynamic_slice_in_dim(x, block * size, size, axis=1)

    def summed(*terms):
        return sum(t.astype(F32) for t in terms).astype(BF16)

    rows = lax.all_gather(activations, "out", axis=0, tiled=True)

    starts = [sum(PARTS[:k]) * height // sum(PARTS) for k in range(len(PARTS))]
    widths = [p * height // sum(PARTS) for p in PARTS]
    shards = [[lax.slice_in_dim(cotangent, s, s + w, axis=1)] for s, w in zip(starts, widths)]
    frontier = []
    state = {}

    def travel(k):
        have = shards[k]
        if len(have) < ring - 1:
            ups, downs = have[max(0, len(have) - 2)], have[-1]
        else:
            half = tokens // 2
            ups, downs = have[-2][:half], have[-1][half:]
        if state.get("loose"):
            state["total"], ups, downs = lax.optimization_barrier((state["total"], ups, downs))
            state["loose"] = False
        if frontier:
            ups, downs = after(ups, *frontier), after(downs, *frontier)
        have += [lax.ppermute(ups, "in", forward), lax.ppermute(downs, "in", backward)]
        return have[-4:-2] if len(have) > 3 else have[:1]

    def multiply(k, total, factor):
        size, tile = widths[k], min(512, width)
        block_rows = sum(PARTS[:k]) // PARTS[k]
        n = ring + 1
        operands = list(shards[k])
        specs = [pl.BlockSpec(x.shape, lambda i, t: (0, 0)) for x in operands]
        operands += [rows] * ring
        specs += [
            pl.BlockSpec((tokens, tile), functools.partial(lambda e, i, t: (t[e], i), e)) for e in range(ring)
        ]
        if out_share % LANES == 0:
            more, more_specs = column_specs(basis_out, out_share, range(ring, ring + outs), size, lambda i: block_rows)
        else:
            fixed = jnp.take(basis_out.reshape(height, outs, out_share), out_block, axis=1).reshape(height, rank)
            more, more_specs = [fixed], [pl.BlockSpec((size, rank), lambda i, t: (block_rows, 0))]
        operands += [*more, factor]
        specs += [*more_specs, pl.BlockSpec((rank, tile), lambda i, t: (0, i))]

        def kernel(table, *refs):
            lefts = [r[...] for r in refs[: n - 2]] + [jnp.concatenate([refs[n - 2][...], refs[n - 1][...]], axis=0)]
            rights = refs[n : n + ring]
            basis = [r[...] for r in refs[n + ring : n + ring + len(more)]]
            basis = basis[0] if len(basis) == 1 else jnp.concatenate(basis, axis=1)
            value = -jnp.dot(basis, refs[n + ring + len(more)][...], preferred_element_type=F32)
            for left, right in zip(lefts, rights):
                value += lax.dot_general(left, right[...], FIRST, preferred_element_type=F32)
            refs[-1][...] = value

        return call(
            kernel, jnp.concatenate([hop, out_block]), operands, specs, (height, width), F32,
            (size, tile), lambda i, t: (block_rows, i), width // tile,
            2 * size * width * (all_tokens + rank), total,
        )


    def coefficients(event):
        if event == "q0":
            part = jnp.dot(activations, basis_in, preferred_element_type=F32).astype(BF16)
            size = tall * in_share
            state["q"] = part_of(part, column, size)
            state["qs"] = [turn_columns(part_of(part, (column + k) % wide, size), k) for k in range(1, wide)]
            return [part]
        if event == "p0":
            x = after(cotangent, *frontier)
            part = jnp.dot(x, basis_out, preferred_element_type=F32).astype(BF16)
            state["p"] = part_of(part, mine, out_share)
            state["ps"] = [swap(part_of(part, mine ^ k, out_share), k) for k in range(1, outs)]
            return [part]
        if event == "q1":
            part = after(summed(state["q"], *state["qs"]), *frontier)
            state["q"] = part_of(part, row, in_share)
            state["qs"] = [turn_rows(part_of(part, (row + k) % tall, in_share), k) for k in range(1, tall)]
            return [part]
        if event == "p1":
            part = after(summed(state["p"], *state["ps"]), *frontier)
            state["ps"] = [part] + [turn_rows(part, k) for k in range(1, tall)]
            return [part]
        if event == "q2":
            part = after(summed(state["q"], *state["qs"]), *frontier)
            state["qs"] = [part] + [swap(part, k) for k in range(1, outs)]
            return [part]
        if event == "p2":
            part = after(jnp.concatenate(state["ps"], axis=0), *frontier)
            state["ps"] = [part] + [turn_columns(part, k) for k in range(1, wide)]
            return [part]
        if event == "c0":
            right = jnp.concatenate(state["qs"], axis=0)
            operands = state["ps"] + [right]
            specs = [pl.BlockSpec(x.shape, lambda i, t: (0, 0)) for x in operands]

            def kernel(table, *refs):
                value = jnp.zeros(refs[-1].shape, F32)
                for e, (a, b) in enumerate(steps):
                    left = refs[b][a * tokens : (a + 1) * tokens, :]
                    at = pl.multiple_of(table[e] * tokens, tokens)
                    value += lax.dot_general(left, refs[wide][pl.ds(at, tokens), :], FIRST, preferred_element_type=F32)
                refs[-1][...] = value.astype(BF16)

            part = call(
                kernel, held_slot, operands, specs, (out_share, in_share), BF16, (out_share, in_share),
                lambda i, t: (0, 0), 1, 2 * all_tokens * out_share * in_share,
            )
            part = after(part, *frontier)
            state["c"] = [part] + [turn_rows(part, k) for k in range(1, tall)]
            return [part]
        if event == "c1":
            part = after(jnp.concatenate(state["c"], axis=1), *frontier)
            state["c"] = [part] + [turn_columns(part, k) for k in range(1, wide)]
            return [part]
        if event == "c2":
            part = after(jnp.concatenate(state["c"], axis=1), *frontier)
            slots = {0: part}
            bit = outs // 2
            slots[bit] = swap(part, bit)
            state["c"] = slots
            for k in (1 << s for s in range(bit.bit_length() - 1)):
                slots[k] = swap(part, k)
            return [part]
        if event == "c3":
            slots = state["c"]
            for k in range(outs):
                if k not in slots:
                    slots[k] = swap(slots[k & ~(k & -k)], k & -k)
            return [slots[outs // 2]]
        cores = [state["c"][k] for k in range(outs)]
        if in_share % LANES == 0:
            more, more_specs = column_specs(basis_in, in_share, range(ring), width, lambda i: 0)
        else:
            more = [jnp.take(basis_in.reshape(width, ring, in_share), in_block, axis=1).reshape(width, rank)]
            more_specs = [pl.BlockSpec((width, rank), lambda i, t: (0, 0))]

        def kernel(table, *refs):
            left = jnp.concatenate([r[...] for r in refs[:outs]], axis=0)
            right = [r[...] for r in refs[outs:-1]]
            right = right[0] if len(right) == 1 else jnp.concatenate(right, axis=1)
            refs[-1][...] = lax.dot_general(left, right, LAST, preferred_element_type=F32).astype(BF16)

        state["f"] = call(
            kernel, in_block, cores + more, [pl.BlockSpec(x.shape, lambda i, t: (0, 0)) for x in cores] + more_specs,
            (rank, width), BF16, (rank, width), lambda i, t: (0, 0), 1, 2 * rank * rank * width,
        )
        return [state["f"]]

    first, later = FIRST_EVENTS, LATER_EVENTS
    if ring // 2 != 4:
        first = [e for e in first if e[0] != "r"]
        later = [e for k in range(len(PARTS)) for e in [f"r{k}"] * (ring // 2) + [f"m{k}"]]
    for event in first:
        frontier = travel(int(event[1])) if event[0] == "r" else coefficients(event)
        if event in ("r0", "r1") and len(shards[int(event[1])]) == 3:
            frontier = []
    state["total"] = None
    for event in later:
        k = int(event[1])
        if event[0] == "r":
            frontier = travel(k)
        else:
            state["total"] = multiply(k, state["total"], state["f"])
            state["loose"] = True
    return state["total"]


def solution(mesh):
    placed = (P("in", "out"), P("out", "in"), P("out", None), P("in", None))
    return jax.shard_map(
        functools.partial(body, *grid_of(mesh)), mesh=mesh, in_specs=placed, out_specs=P("out", "in"), check_vma=False
    )
```

```python
import functools

import jax
import jax.numpy as jnp
import numpy as np
from jax import lax
from jax.experimental import pallas as pl
from jax.experimental.pallas import tpu as pltpu
from jax.sharding import PartitionSpec as P

TOKENS_FIRST = (((0,), (0,)), ((), ()))
LAST_LAST = (((1,), (1,)), ((), ()))
F32, BF16 = jnp.float32, jnp.bfloat16


def ring_order(mesh):
    count = mesh.shape["in"]
    places = [d.coords for d in mesh.devices[0]]
    wide = sum(p[2] == places[0][2] for p in places)
    tall = count // wide
    if wide < 2 or tall % 2:
        return list(range(count))
    order = []
    for row in range(tall):
        columns = range(1, wide) if row % 2 == 0 else range(wide - 1, 0, -1)
        order += [row * wide + column for column in columns]
    return order + [row * wide for row in reversed(range(tall))]


def add_products(offsets, shards, rows_of, low, high, total=None, removal=None, first=0, count=None, tile=512):
    height, width = high, rows_of.shape[1]
    count = height if count is None else count
    tile = min(tile, count)
    tokens = shards[0][0].shape[0]

    def kernel(offsets_ref, *refs):
        n = len(shards)
        value = None
        for left, right in zip(refs[:n], refs[n : 2 * n]):
            term = lax.dot_general(left[...], right[...], TOKENS_FIRST, preferred_element_type=F32)
            value = term if value is None else value + term
        rest = refs[2 * n : -1]
        if removal is not None:
            value = value - jnp.dot(rest[0][...], rest[1][...], preferred_element_type=F32)
        if total is not None:
            value = value + rest[-1][...]
        refs[-1][...] = value.astype(refs[-1].dtype)

    operands = [s[0] for s in shards] + [rows_of] * len(shards)
    specs = [
        pl.BlockSpec((tokens, tile), functools.partial(lambda start, i, offs: (0, start + i), s[1] // tile))
        for s in shards
    ]
    specs += [
        pl.BlockSpec((tokens, width), functools.partial(lambda entry, i, offs: (offs[entry], 0), s[2]))
        for s in shards
    ]
    base = first // tile
    if removal is not None:
        operands += list(removal)
        specs += [
            pl.BlockSpec((tile, removal[0].shape[1]), lambda i, offs: (base + i, 0)),
            pl.BlockSpec(removal[1].shape, lambda i, offs: (0, 0)),
        ]
    aliases = {}
    if total is not None:
        operands.append(total)
        specs.append(pl.BlockSpec((tile, width), lambda i, offs: (base + i, 0)))
        aliases = {len(operands): 0}
    depth = tokens * len(shards) + (removal[0].shape[1] if removal is not None else 0)
    return pl.pallas_call(
        kernel,
        out_shape=jax.ShapeDtypeStruct((height, width), low),
        grid_spec=pltpu.PrefetchScalarGridSpec(
            num_scalar_prefetch=1,
            grid=(count // tile,),
            in_specs=specs,
            out_specs=pl.BlockSpec((tile, width), lambda i, offs: (base + i, 0)),
        ),
        input_output_aliases=aliases,
        compiler_params=pltpu.CompilerParams(vmem_limit_bytes=60 * 2**20),
        cost_estimate=pl.CostEstimate(
            flops=2 * count * width * depth,
            bytes_accessed=count * width * (8 if total is not None else 4) + depth * (count + width) * 2,
            transcendentals=0,
        ),
    )(offsets, *operands)


def stacked(parts):
    rows, width = parts[0].shape
    tile = min(512, width)

    def kernel(*refs):
        for k, r in enumerate(refs[:-1]):
            refs[-1][k * rows : (k + 1) * rows, :] = r[...]

    return pl.pallas_call(
        kernel,
        out_shape=jax.ShapeDtypeStruct((rows * len(parts), width), parts[0].dtype),
        grid=(width // tile,),
        in_specs=[pl.BlockSpec((rows, tile), lambda i: (0, i))] * len(parts),
        out_specs=pl.BlockSpec((rows * len(parts), tile), lambda i: (0, i)),
        compiler_params=pltpu.CompilerParams(vmem_limit_bytes=60 * 2**20),
    )(*parts)


def after(x, *others):
    return lax.optimization_barrier((x, *others))[0]


def body(order, cotangent, activations, basis_out, basis_in):
    ring = len(order)
    outs = lax.axis_size("out")
    forward = [(order[k], order[(k + 1) % ring]) for k in range(ring)]
    backward = [(b, a) for a, b in forward]

    def up(x):
        return lax.ppermute(x, "in", forward)

    def down(x):
        return lax.ppermute(x, "in", backward)

    here, mine = lax.axis_index("in"), lax.axis_index("out")
    per = ring // outs
    hops = [0] + [d for s in range(1, ring // 2) for d in (-s, s)] + [ring // 2]
    lines = [
        [((j // per) ^ o) * per + j % per for j in (order[(order.index(i) + d) % ring] for d in hops)]
        for o in range(outs)
        for i in range(ring)
    ]
    offsets = lax.dynamic_index_in_dim(jnp.asarray(np.asarray(lines, np.int32)), mine * ring + here, keepdims=False)

    height = cotangent.shape[1]
    ups, downs = up(cotangent), down(cotangent)
    shards = [(cotangent, 0, 0), (ups, 0, 1), (downs, 0, 2)]

    share = lax.psum_scatter(
        jnp.dot(cotangent, basis_out, preferred_element_type=F32).astype(BF16),
        "out", scatter_dimension=1, tiled=True,
    )
    coefficients = lax.all_gather(share, "in", axis=0, tiled=True)

    slots = {0: activations}
    bit = outs // 2
    while bit:
        swap = [(i, i ^ bit) for i in range(outs)]
        slots.update({k ^ bit: lax.ppermute(v, "out", swap) for k, v in slots.items()})
        bit //= 2
    rows = stacked([slots[k] for k in range(outs)])

    coefficients = after(coefficients, ups, downs, rows)
    block = coefficients.shape[0] // outs
    coefficients = jnp.concatenate(
        [lax.dynamic_slice_in_dim(coefficients, (mine ^ k) * block, block, axis=0) for k in range(outs)], axis=0
    )
    seen = lax.dot_general(coefficients, rows, TOKENS_FIRST, preferred_element_type=F32).astype(BF16)
    core_part = jnp.dot(seen, basis_in, preferred_element_type=F32).astype(BF16)
    core = lax.psum(core_part, "in")

    total = None
    for step in range(2, ring // 2):
        ups, downs = up(ups), down(downs)
        if step == 2:
            ups, downs, _ = lax.optimization_barrier((ups, downs, core_part))
        shards += [(ups, 0, 2 * step - 1), (downs, 0, 2 * step)]
        if step == 2:
            first = len(shards)
            total = add_products(offsets, shards, rows, F32, height)
    ups, downs, total = lax.optimization_barrier((ups, downs, total))
    half = height // 2
    last = [up(ups[:, :half]), down(downs[:, half:])]
    rest = shards[first:-2] + [(ups, 0, ring - 3), (downs, 0, ring - 2)] if first < len(shards) else []
    core = after(core, ups, downs)
    if rest:
        total = add_products(offsets, rest, rows, F32, height, total, None, 0, half)
    core, total = lax.optimization_barrier((core, total))
    core = lax.all_gather(core, "out", axis=0, tiled=True)
    if rest:
        rest = [(x, half, e) for x, _, e in rest]
        total = add_products(offsets, rest, rows, F32, height, total, None, half, half)
    core, total = lax.optimization_barrier((core, total))
    factor = jnp.dot(core, basis_in.T, preferred_element_type=F32).astype(BF16)
    return remove(offsets, last, rows, total, basis_out, factor, ring - 1)


def remove(offsets, last, rows, total, basis, factor, entry):
    height, width = total.shape
    tokens, half = last[0].shape
    tile = min(256, width)
    rank = factor.shape[0]
    once = pl.Buffered(1)

    def kernel(offsets_ref, left_ref, right_ref, rows_ref, basis_ref, factor_ref, total_ref, out_ref, turned_ref):
        @pl.when(pl.program_id(0) == 0)
        def _():
            turned_ref[:half, :] = left_ref[...].T
            turned_ref[half:, :] = right_ref[...].T

        value = total_ref[...] - jnp.dot(basis_ref[...], factor_ref[...], preferred_element_type=F32)
        out_ref[...] = value + jnp.dot(turned_ref[...], rows_ref[...], preferred_element_type=F32)

    return pl.pallas_call(
        kernel,
        out_shape=jax.ShapeDtypeStruct((height, width), F32),
        grid_spec=pltpu.PrefetchScalarGridSpec(
            num_scalar_prefetch=1,
            grid=(width // tile,),
            in_specs=[
                pl.BlockSpec((tokens, half), lambda i, offs: (0, 0), pipeline_mode=once),
                pl.BlockSpec((tokens, half), lambda i, offs: (0, 0), pipeline_mode=once),
                pl.BlockSpec((tokens, tile), lambda i, offs: (offs[entry], i)),
                pl.BlockSpec((height, rank), lambda i, offs: (0, 0), pipeline_mode=once),
                pl.BlockSpec((rank, tile), lambda i, offs: (0, i)),
                pl.BlockSpec((height, tile), lambda i, offs: (0, i)),
            ],
            out_specs=pl.BlockSpec((height, tile), lambda i, offs: (0, i)),
            scratch_shapes=[pltpu.VMEM((height, tokens), BF16)],
        ),
        input_output_aliases={6: 0},
        compiler_params=pltpu.CompilerParams(vmem_limit_bytes=60 * 2**20),
    )(offsets, last[0], last[1], rows, basis, factor, total)


def solution(mesh):
    placed = (P("in", "out"), P("out", "in"), P("out", None), P("in", None))
    return jax.shard_map(
        functools.partial(body, ring_order(mesh)), mesh=mesh, in_specs=placed, out_specs=P("out", "in"), check_vma=False
    )
```

```python
import functools

import jax
import jax.numpy as jnp
import numpy as np
from jax import lax
from jax.experimental import pallas as pl
from jax.experimental.pallas import tpu as pltpu
from jax.sharding import PartitionSpec as P

TOKENS_FIRST = (((0,), (0,)), ((), ()))
LAST_LAST = (((1,), (1,)), ((), ()))
F32, BF16 = jnp.float32, jnp.bfloat16


def ring_order(mesh):
    count = mesh.shape["in"]
    places = [d.coords for d in mesh.devices[0]]
    wide = sum(p[2] == places[0][2] for p in places)
    tall = count // wide
    if wide < 2 or tall % 2:
        return list(range(count))
    order = []
    for row in range(tall):
        columns = range(1, wide) if row % 2 == 0 else range(wide - 1, 0, -1)
        order += [row * wide + column for column in columns]
    return order + [row * wide for row in reversed(range(tall))]


def add_products(offsets, shards, rows_of, low, high, total=None, removal=None, first=0, count=None, tile=512):
    height, width = high, rows_of.shape[1]
    count = height if count is None else count
    tile = min(tile, count)
    tokens = shards[0][0].shape[0]

    def kernel(offsets_ref, *refs):
        n = len(shards)
        value = None
        for left, right in zip(refs[:n], refs[n : 2 * n]):
            term = lax.dot_general(left[...], right[...], TOKENS_FIRST, preferred_element_type=F32)
            value = term if value is None else value + term
        rest = refs[2 * n : -1]
        if removal is not None:
            value = value - jnp.dot(rest[0][...], rest[1][...], preferred_element_type=F32)
        if total is not None:
            value = value + rest[-1][...]
        refs[-1][...] = value.astype(refs[-1].dtype)

    operands = [s[0] for s in shards] + [rows_of] * len(shards)
    specs = [
        pl.BlockSpec((tokens, tile), functools.partial(lambda start, i, offs: (0, start + i), s[1] // tile))
        for s in shards
    ]
    specs += [
        pl.BlockSpec((tokens, width), functools.partial(lambda entry, i, offs: (offs[entry], 0), s[2]))
        for s in shards
    ]
    base = first // tile
    if removal is not None:
        operands += list(removal)
        specs += [
            pl.BlockSpec((tile, removal[0].shape[1]), lambda i, offs: (base + i, 0)),
            pl.BlockSpec(removal[1].shape, lambda i, offs: (0, 0)),
        ]
    aliases = {}
    if total is not None:
        operands.append(total)
        specs.append(pl.BlockSpec((tile, width), lambda i, offs: (base + i, 0)))
        aliases = {len(operands): 0}
    depth = tokens * len(shards) + (removal[0].shape[1] if removal is not None else 0)
    return pl.pallas_call(
        kernel,
        out_shape=jax.ShapeDtypeStruct((height, width), low),
        grid_spec=pltpu.PrefetchScalarGridSpec(
            num_scalar_prefetch=1,
            grid=(count // tile,),
            in_specs=specs,
            out_specs=pl.BlockSpec((tile, width), lambda i, offs: (base + i, 0)),
        ),
        input_output_aliases=aliases,
        compiler_params=pltpu.CompilerParams(vmem_limit_bytes=60 * 2**20),
        cost_estimate=pl.CostEstimate(
            flops=2 * count * width * depth,
            bytes_accessed=count * width * (8 if total is not None else 4) + depth * (count + width) * 2,
            transcendentals=0,
        ),
    )(offsets, *operands)


def stacked(parts):
    rows, width = parts[0].shape
    tile = min(512, width)

    def kernel(*refs):
        for k, r in enumerate(refs[:-1]):
            refs[-1][k * rows : (k + 1) * rows, :] = r[...]

    return pl.pallas_call(
        kernel,
        out_shape=jax.ShapeDtypeStruct((rows * len(parts), width), parts[0].dtype),
        grid=(width // tile,),
        in_specs=[pl.BlockSpec((rows, tile), lambda i: (0, i))] * len(parts),
        out_specs=pl.BlockSpec((rows * len(parts), tile), lambda i: (0, i)),
        compiler_params=pltpu.CompilerParams(vmem_limit_bytes=60 * 2**20),
    )(*parts)


def after(x, *others):
    return lax.optimization_barrier((x, *others))[0]


def body(order, cotangent, activations, basis_out, basis_in):
    ring = len(order)
    outs = lax.axis_size("out")
    forward = [(order[k], order[(k + 1) % ring]) for k in range(ring)]
    backward = [(b, a) for a, b in forward]

    def up(x):
        return lax.ppermute(x, "in", forward)

    def down(x):
        return lax.ppermute(x, "in", backward)

    here, mine = lax.axis_index("in"), lax.axis_index("out")
    per = ring // outs
    hops = [0] + [d for s in range(1, ring // 2) for d in (-s, s)] + [ring // 2]
    lines = [
        [((j // per) ^ o) * per + j % per for j in (order[(order.index(i) + d) % ring] for d in hops)]
        for o in range(outs)
        for i in range(ring)
    ]
    offsets = lax.dynamic_index_in_dim(jnp.asarray(np.asarray(lines, np.int32)), mine * ring + here, keepdims=False)

    height = cotangent.shape[1]
    ups, downs = up(cotangent), down(cotangent)
    shards = [(cotangent, 0, 0), (ups, 0, 1), (downs, 0, 2)]

    share = lax.psum_scatter(
        jnp.dot(cotangent, basis_out, preferred_element_type=F32).astype(BF16),
        "out", scatter_dimension=1, tiled=True,
    )
    coefficients = lax.all_gather(share, "in", axis=0, tiled=True)

    slots = {0: activations}
    bit = outs // 2
    while bit:
        swap = [(i, i ^ bit) for i in range(outs)]
        slots.update({k ^ bit: lax.ppermute(v, "out", swap) for k, v in slots.items()})
        bit //= 2
    rows = stacked([slots[k] for k in range(outs)])

    coefficients = after(coefficients, ups, downs, rows, offsets)
    block = coefficients.shape[0] // outs
    coefficients = jnp.concatenate(
        [lax.dynamic_slice_in_dim(coefficients, (mine ^ k) * block, block, axis=0) for k in range(outs)], axis=0
    )
    seen = lax.dot_general(coefficients, rows, TOKENS_FIRST, preferred_element_type=F32).astype(BF16)
    core_part = jnp.dot(seen, basis_in, preferred_element_type=F32).astype(BF16)
    core = lax.psum(core_part, "in")

    total = None
    for step in range(2, ring // 2):
        ups, downs = up(ups), down(downs)
        if step == 2:
            ups, downs, _ = lax.optimization_barrier((ups, downs, core_part))
        shards += [(ups, 0, 2 * step - 1), (downs, 0, 2 * step)]
        if step == 2:
            first = len(shards)
            total = add_products(offsets, shards, rows, F32, height)
    ups, downs, total = lax.optimization_barrier((ups, downs, total))
    half = height // 2
    last = [up(ups[:, :half]), down(downs[:, half:])]
    rest = shards[first:-2] + [(ups, 0, ring - 3), (downs, 0, ring - 2)] if first < len(shards) else []
    core = after(core, ups, downs)
    if rest:
        total = add_products(offsets, rest, rows, F32, height, total, None, 0, half)
    core, total = lax.optimization_barrier((core, total))
    core = lax.all_gather(core, "out", axis=0, tiled=True)
    if rest:
        rest = [(x, half, e) for x, _, e in rest]
        total = add_products(offsets, rest, rows, F32, height, total, None, half, half)
    core, total = lax.optimization_barrier((core, total))
    factor = jnp.dot(core, basis_in.T, preferred_element_type=F32).astype(BF16)
    return remove(offsets, last, rows, total, basis_out, factor, ring - 1)


def remove(offsets, last, rows, total, basis, factor, entry):
    height, width = total.shape
    tokens, half = last[0].shape
    tile = min(256, width)
    rank = factor.shape[0]
    once = pl.Buffered(1)

    def kernel(offsets_ref, left_ref, right_ref, rows_ref, basis_ref, factor_ref, total_ref, out_ref, turned_ref):
        @pl.when(pl.program_id(0) == 0)
        def _():
            turned_ref[:half, :] = left_ref[...].T
            turned_ref[half:, :] = right_ref[...].T

        value = total_ref[...] - jnp.dot(basis_ref[...], factor_ref[...], preferred_element_type=F32)
        out_ref[...] = value + jnp.dot(turned_ref[...], rows_ref[...], preferred_element_type=F32)

    return pl.pallas_call(
        kernel,
        out_shape=jax.ShapeDtypeStruct((height, width), F32),
        grid_spec=pltpu.PrefetchScalarGridSpec(
            num_scalar_prefetch=1,
            grid=(width // tile,),
            in_specs=[
                pl.BlockSpec((tokens, half), lambda i, offs: (0, 0), pipeline_mode=once),
                pl.BlockSpec((tokens, half), lambda i, offs: (0, 0), pipeline_mode=once),
                pl.BlockSpec((tokens, tile), lambda i, offs: (offs[entry], i)),
                pl.BlockSpec((height, rank), lambda i, offs: (0, 0), pipeline_mode=once),
                pl.BlockSpec((rank, tile), lambda i, offs: (0, i)),
                pl.BlockSpec((height, tile), lambda i, offs: (0, i)),
            ],
            out_specs=pl.BlockSpec((height, tile), lambda i, offs: (0, i)),
            scratch_shapes=[pltpu.VMEM((height, tokens), BF16)],
        ),
        input_output_aliases={6: 0},
        compiler_params=pltpu.CompilerParams(vmem_limit_bytes=60 * 2**20),
    )(offsets, last[0], last[1], rows, basis, factor, total)


def solution(mesh):
    placed = (P("in", "out"), P("out", "in"), P("out", None), P("in", None))
    return jax.shard_map(
        functools.partial(body, ring_order(mesh)), mesh=mesh, in_specs=placed, out_specs=P("out", "in"), check_vma=False
    )
```
